512 devices in a mesh: corpus: 256 (over z_lo, y, x, core), feat: 2 (over z_hi).
Axes of the slice: x: 4, y: 8, z: 8 (z_hi: 2, z_lo: 4; z = z_hi * 4 + z_lo), core: 2. Of those that a mesh axis runs over, the one named last changes fastest.
Arguments:
- fresh_embed: bfloat16 [65536, 1024], P('corpus', 'feat'), may hold values from -64 to 64
- replay_embed: bfloat16 [524288, 1024], P('corpus', 'feat'), may hold values from -64 to 64
Outputs:
- fresh_lse: float32 [65536], P('corpus')
- replay_lse: float32 [524288], P(('corpus', 'feat'))
The draws below stay inside these ranges and needn't reach their ends.
All inputs are finite; a program needn't handle non-finite values.
Results may differ from the reference program's by a relative error of at most 0.0003.
Values may be sent and summed in bfloat16 or wider, within the bound.
A program may use at most 64 MiB of HBM per device.

```python
import math
import jax
import jax.numpy as jnp
from jax import lax

E = 1024
WINDOW = 8
F_DEV = 256
R_DEV = 2048
FRESH = 65536
REPLAY = 524288
N_CORPUS = 256


def row_scales(key, row_count, widest):
    picked = jax.random.uniform(jax.random.fold_in(key, 5), (row_count, 1), jnp.float32)
    return jnp.exp(picked * math.log(widest))


def draw_fresh_embed(key, part):
    key = jax.random.fold_in(key, 3)
    entries = jnp.clip(jax.random.normal(key, (FRESH, E), jnp.float32), -4.5, 4.5)
    values = entries * row_scales(key, FRESH, 10.0)
    return values.astype(jnp.bfloat16)


def draw_replay_embed(key, part):
    key = jax.random.fold_in(key, 4)
    entries = jnp.clip(jax.random.normal(key, (REPLAY, E), jnp.float32), -4.5, 4.5)
    values = entries * row_scales(key, REPLAY, 10.0)
    return values.astype(jnp.bfloat16)


def setup_inputs(seed: int = 0) -> dict:
    keys = jax.random.split(jax.random.key(seed), 3)
    return {
        "fresh_embed": draw_fresh_embed(jax.random.fold_in(keys[2], 71), 0),
        "replay_embed": draw_replay_embed(jax.random.fold_in(keys[2], 71), 0),
    }


NEG_FLOOR = -1e+30

def reference(fresh_embed, replay_embed):
    full_width = fresh_embed.shape[1]
    score_scale = 0.25 / math.sqrt(full_width)
    fresh_blocks = fresh_embed.astype(jnp.float32).reshape(N_CORPUS, F_DEV, full_width)
    key_slabs = replay_embed.astype(jnp.float32).reshape(N_CORPUS, R_DEV, full_width)
    offsets = jnp.arange(WINDOW, dtype=jnp.int32) - (WINDOW // 2 - 1)
    slab_ids = jnp.arange(N_CORPUS, dtype=jnp.int32)

    def visit_slab(carried, inputs):
        row_max, row_total = carried
        slab_id, keys_block = inputs
        block_ids = ((slab_id + offsets) % N_CORPUS).astype(jnp.int32)
        queries = fresh_blocks[block_ids].reshape(WINDOW * F_DEV, full_width)
        scores = jnp.dot(queries, keys_block.T, precision=lax.Precision.HIGHEST) * score_scale
        column_max = lax.optimization_barrier(jnp.max(scores, axis=0))
        column_lse = column_max + jnp.log(lax.optimization_barrier(jnp.sum(jnp.exp(scores - column_max[None, :]), axis=0)))
        tile_max = lax.optimization_barrier(jnp.max(scores, axis=1))
        tile_total = lax.optimization_barrier(jnp.sum(jnp.exp(scores - tile_max[:, None]), axis=1))
        tile_max = tile_max.reshape(WINDOW, F_DEV)
        tile_total = tile_total.reshape(WINDOW, F_DEV)
        old_max = row_max[block_ids]
        old_total = row_total[block_ids]
        next_max = jnp.maximum(old_max, tile_max)
        next_total = old_total * jnp.exp(old_max - next_max) + tile_total * jnp.exp(tile_max - next_max)
        row_max = row_max.at[block_ids].set(next_max)
        row_total = row_total.at[block_ids].set(next_total)
        return ((row_max, row_total), column_lse)
    initial = (jnp.full((N_CORPUS, F_DEV), NEG_FLOOR, jnp.float32), jnp.zeros((N_CORPUS, F_DEV), jnp.float32))
    (row_max, row_total), column_lse = lax.scan(visit_slab, initial, (slab_ids, key_slabs))
    return ((row_max + jnp.log(row_total)).reshape(FRESH), column_lse.reshape(REPLAY))
```

```python
import functools
import math

import jax
import jax.numpy as jnp
from jax import lax
from jax.experimental import pallas as pl
from jax.experimental.pallas import tpu as pltpu
from jax.sharding import PartitionSpec as P

MESH = pl.DeviceIdType.MESH
WINDOW = 8
BEHIND = 3
OWN = 3
NEG_FLOOR = -1e30
LN2 = math.log(2.0)


def kernel(
    corpus,
    steps,
    scale,
    fresh_ref,
    replay_ref,
    fresh_out,
    replay_out,
    blocks,
    slab,
    scores,
    fresh_max,
    fresh_sum,
    stats,
    landed,
    local_sem,
    zf_send,
    zf_recv,
    zr_send,
    zr_recv,
    out_send,
    share_send,
    block_recv,
    stat_send,
    stat_recv,
):
    rows, half = fresh_ref.shape
    share = replay_ref.shape[0] // 2
    step_rows = share // steps
    me_c = lax.axis_index("corpus")
    me_f = lax.axis_index("feat")
    core = lax.rem(me_c, 2)
    ring = 2 * corpus
    me = me_f * corpus + me_c

    def device(offset):
        there = lax.rem(me + offset + ring, ring)
        return (lax.rem(there, corpus), there // corpus)

    def block(slot):
        return pl.ds(pl.multiple_of(slot * rows, rows), rows)

    def columns(feature_half):
        return pl.ds(pl.multiple_of(feature_half * half, half), half)

    partner = device(corpus)
    twin = device(1 - 2 * core)
    mine = columns(me_f)
    other = columns(1 - me_f)

    barrier = pltpu.get_barrier_semaphore()
    offsets = [o + p for p in (0, corpus) for o in range(-4, 5) if o + p]
    for offset in offsets:
        pl.semaphore_signal(
            barrier, inc=1, device_id=device(offset), device_id_type=MESH
        )
    pl.semaphore_wait(barrier, len(offsets))

    z_fresh = pltpu.make_async_remote_copy(
        src_ref=fresh_ref,
        dst_ref=blocks.at[block(OWN), mine],
        send_sem=zf_send,
        recv_sem=zf_recv,
        device_id=partner,
        device_id_type=MESH,
    )
    z_fresh.start()

    def z_replay(step):
        at = pl.multiple_of(step * step_rows, step_rows)
        return pltpu.make_async_remote_copy(
            src_ref=replay_ref.at[
                pl.ds(pl.multiple_of((1 - me_f) * share + at, step_rows), step_rows), :
            ],
            dst_ref=slab.at[pl.ds(at, step_rows), mine],
            send_sem=zr_send.at[step],
            recv_sem=zr_recv.at[step],
            device_id=partner,
            device_id_type=MESH,
        )

    own_fresh = pltpu.make_async_copy(
        fresh_ref, blocks.at[block(OWN), mine], local_sem.at[0]
    )
    own_replay = pltpu.make_async_copy(
        replay_ref.at[pl.ds(pl.multiple_of(me_f * share, share), share), :],
        slab.at[:, mine],
        local_sem.at[1],
    )
    own_fresh.start()
    own_replay.start()

    def spread(phase, index, source, cols, target, slot):
        return pltpu.make_async_remote_copy(
            src_ref=source,
            dst_ref=blocks.at[block(slot), cols],
            send_sem=out_send.at[phase, index],
            recv_sem=block_recv.at[phase, slot],
            device_id=target,
            device_id_type=MESH,
        )

    def outgoing(phase):
        cols = mine if phase == 0 else other
        source = fresh_ref if phase == 0 else blocks.at[block(OWN), cols]
        always = [
            spread(phase, 0, source, cols, device(-2), 5),
            spread(phase, 1, source, cols, device(2), 1),
            spread(phase, 2, source, cols, device(-4), 7),
            spread(phase, 3, source, cols, twin, 2 + 2 * core),
        ]
        return always, spread(phase, 4, source, cols, device(3), 0)

    def sharing(phase, index, slot, to):
        from_feat = device(slot - BEHIND)[1]
        cols = columns(from_feat if phase == 0 else 1 - from_feat)
        return pltpu.make_async_remote_copy(
            src_ref=blocks.at[block(slot), cols],
            dst_ref=blocks.at[block(to), cols],
            send_sem=share_send.at[phase, index],
            recv_sem=block_recv.at[phase, to],
            device_id=twin,
            device_id_type=MESH,
        )

    def arrival(phase, slot):
        pltpu.make_async_copy(
            blocks.at[block(slot), mine],
            blocks.at[block(slot), mine],
            block_recv.at[phase, slot],
        ).wait()

    def start_spread(phase):
        always, odd = outgoing(phase)
        for copy in always:
            copy.start()

        @pl.when(core == 1)
        def _():
            odd.start()

    def start_sharing(phase):
        for index, slot in enumerate((1, 5)):
            arrival(phase, slot)
            sharing(phase, index, slot, slot - 1 + 2 * core).start()
        arrival(phase, 7)

        @pl.when(core == 0)
        def _():
            sharing(phase, 2, 7, 6).start()

    def finish_spread(phase):
        always, odd = outgoing(phase)
        for copy in always:
            copy.wait_send()

        @pl.when(core == 1)
        def _():
            odd.wait_send()

        for index, slot in enumerate((1, 5)):
            sharing(phase, index, slot, slot - 1 + 2 * core).wait_send()

        @pl.when(core == 0)
        def _():
            sharing(phase, 2, 7, 6).wait_send()

    start_spread(0)
    z_fresh.wait()

    def start_replay(step, carry):
        z_replay(step).start()
        return carry

    lax.fori_loop(0, steps, start_replay, 0)
    start_spread(1)

    fresh_max[...] = jnp.full_like(fresh_max, NEG_FLOOR)
    fresh_sum[...] = jnp.zeros_like(fresh_sum)
    stats[...] = jnp.zeros_like(stats)

    for phase in (0, 1):
        start_sharing(phase)
    for phase in (0, 1):
        for slot in (0, 2, 4, 6):
            arrival(phase, slot)
    own_fresh.wait()
    own_replay.wait()

    groups = step_rows // 8
    chunk_rows = step_rows // 128

    def visit(step, carry):
        z_replay(step).wait_recv()
        at = pl.multiple_of(step * step_rows, step_rows)
        row_max = jnp.full((step_rows, 128), NEG_FLOOR, jnp.float32)
        for k in range(WINDOW):
            score = (
                lax.dot_general(
                    slab[pl.ds(at, step_rows), :],
                    blocks[k * rows : (k + 1) * rows, :],
                    (((1,), (1,)), ((), ())),
                    preferred_element_type=jnp.float32,
                )
                * scale
            )
            scores[:, k * rows : (k + 1) * rows] = score
            for j in range(rows // 128):
                row_max = jnp.maximum(row_max, score[:, j * 128 : (j + 1) * 128])
            grouped = score.reshape(groups, 8, rows)
            old = fresh_max[:, k * rows : (k + 1) * rows]
            new = jnp.maximum(old, jnp.max(grouped, axis=0))
            fresh_max[:, k * rows : (k + 1) * rows] = new
            fresh_sum[:, k * rows : (k + 1) * rows] = fresh_sum[
                :, k * rows : (k + 1) * rows
            ] * jnp.exp2(old - new) + jnp.sum(jnp.exp2(grouped - new[None]), axis=0)
        row_sum = jnp.zeros((step_rows, 128), jnp.float32)
        for j in range(WINDOW * rows // 128):
            row_sum += jnp.exp2(scores[:, j * 128 : (j + 1) * 128] - row_max)
        row_max = row_max.T
        row_sum = row_sum.T
        top = jnp.max(row_max, axis=0, keepdims=True)
        total = jnp.sum(row_sum * jnp.exp2(row_max - top), axis=0, keepdims=True)
        result = LN2 * (top + jnp.log2(total))
        for j in range(chunk_rows):
            replay_out[pl.ds(step * chunk_rows + j, 1), :] = result[
                :, j * 128 : (j + 1) * 128
            ]
        return carry

    lax.fori_loop(0, steps, visit, 0)

    for k in range(WINDOW):
        span = slice(k * rows, (k + 1) * rows)
        top = jnp.max(fresh_max[:, span], axis=0, keepdims=True)
        total = jnp.sum(
            fresh_sum[:, span] * jnp.exp2(fresh_max[:, span] - top),
            axis=0,
            keepdims=True,
        )
        for j in range(rows // 128):
            stats[k, j : j + 1, :] = top[:, j * 128 : (j + 1) * 128]
            stats[k, 2 + j : 3 + j, :] = total[:, j * 128 : (j + 1) * 128]

    def send_stats(k, side):
        return pltpu.make_async_remote_copy(
            src_ref=stats.at[k],
            dst_ref=landed.at[side, k],
            send_sem=stat_send.at[side, k],
            recv_sem=stat_recv.at[side, k],
            device_id=device(k - BEHIND + side * corpus),
            device_id_type=MESH,
        )

    outward = [
        (k, side) for side in (1, 0) for k in range(WINDOW) if side or k != BEHIND
    ]
    for k, side in outward:
        send_stats(k, side).start()
    landed[0, BEHIND] = stats[BEHIND]
    for phase in (0, 1):
        finish_spread(phase)

    def end_replay(step, carry):
        z_replay(step).wait_send()
        return carry

    lax.fori_loop(0, steps, end_replay, 0)
    for k, side in outward:
        send_stats(k, side).wait()
    got = landed[...].reshape(2 * WINDOW, 8, 128)
    top = jnp.max(got[:, 0:2, :], axis=0)
    total = jnp.sum(got[:, 2:4, :] * jnp.exp2(got[:, 0:2, :] - top[None]), axis=0)
    fresh_out[...] = LN2 * (top + jnp.log2(total))


def per_device(corpus, fresh_embed, replay_embed):
    rows, half = fresh_embed.shape
    share = replay_embed.shape[0] // 2
    steps = 4
    step_rows = share // steps
    full = 2 * half
    scale = 0.25 / math.sqrt(full) * math.log2(math.e)
    dma = pltpu.SemaphoreType.DMA
    fresh_lse, replay_lse = pl.pallas_call(
        functools.partial(kernel, corpus, steps, scale),
        out_shape=(
            jax.ShapeDtypeStruct((rows // 128, 128), jnp.float32),
            jax.ShapeDtypeStruct((share // 128, 128), jnp.float32),
        ),
        in_specs=[pl.BlockSpec(memory_space=pl.ANY)] * 2,
        out_specs=[pl.BlockSpec(memory_space=pltpu.VMEM)] * 2,
        scratch_shapes=[
            pltpu.VMEM((WINDOW * rows, full), jnp.bfloat16),
            pltpu.VMEM((share, full), jnp.bfloat16),
            pltpu.VMEM((step_rows, WINDOW * rows), jnp.float32),
            pltpu.VMEM((8, WINDOW * rows), jnp.float32),
            pltpu.VMEM((8, WINDOW * rows), jnp.float32),
            pltpu.VMEM((WINDOW, 8, 128), jnp.float32),
            pltpu.VMEM((2, WINDOW, 8, 128), jnp.float32),
            dma((2,)),
            dma,
            dma,
            dma((steps,)),
            dma((steps,)),
            dma((2, 5)),
            dma((2, 3)),
            dma((2, WINDOW)),
            dma((2, WINDOW)),
            dma((2, WINDOW)),
        ],
        compiler_params=pltpu.CompilerParams(
            collective_id=0, has_side_effects=True, vmem_limit_bytes=40 * 2**20
        ),
    )(fresh_embed, replay_embed)
    return fresh_lse.reshape(rows), replay_lse.reshape(share)


def solution(mesh):
    placed = (P("corpus", "feat"), P("corpus", "feat"))
    return jax.shard_map(
        functools.partial(per_device, mesh.shape["corpus"]),
        mesh=mesh,
        in_specs=placed,
        out_specs=(P("corpus"), P(("corpus", "feat"))),
        check_vma=False,
    )
```

```python
import functools
import math

import jax
import jax.numpy as jnp
from jax import lax
from jax.experimental import pallas as pl
from jax.experimental.pallas import tpu as pltpu
from jax.sharding import PartitionSpec as P

MESH = pl.DeviceIdType.MESH
WINDOW = 8
BEHIND = 3
OWN = 3
PLANE = 64
PIECES = 8
NEG_FLOOR = -1e30
LN2 = math.log(2.0)


def kernel(
    corpus,
    plane,
    chunks,
    first_steps,
    scale,
    fresh_ref,
    replay_ref,
    fresh_out,
    replay_out,
    blocks,
    slab,
    scores,
    fresh_max,
    fresh_sum,
    stats,
    landed,
    carried,
    local_sem,
    zf_send,
    zf_recv,
    zr_send,
    zr_recv,
    out_send,
    pass_send,
    edge_send,
    block_recv,
    swap_send,
    carry_send,
    carry_recv,
    stat_send,
    stat_recv,
):
    rows, half = fresh_ref.shape
    share = replay_ref.shape[0] // 2
    lanes = plane // PIECES
    piece = rows // PIECES
    me_c = lax.axis_index("corpus")
    me_f = lax.axis_index("feat")
    ring = 2 * corpus
    me = me_f * corpus + me_c
    here = lax.rem(me_c, plane)
    core = lax.rem(here, 2)
    column = lax.rem(here, lanes) // 2
    row = here // lanes

    def device(offset):
        there = lax.rem(me + offset + ring, ring)
        return (lax.rem(there, corpus), there // corpus)

    def block(slot):
        return pl.ds(pl.multiple_of(slot * rows, rows), rows)

    def columns(feature_half):
        return pl.ds(pl.multiple_of(feature_half * half, half), half)

    partner = device(corpus)
    twin = device(1 - 2 * core)
    mine = columns(me_f)
    other = columns(1 - me_f)
    low = here < 2
    high = here >= plane - 2
    back_source = here < 4
    ahead_source = here >= plane - 3
    carries_back = column < 2
    carries = jnp.logical_or(column != 2, core == 1)

    def carrier(p):
        there = p * lanes + 2 * column + core
        return device(there - here + jnp.where(back_source, -plane, plane))

    goal = jnp.where(
        carries_back,
        plane - 2 + core,
        jnp.where(column == 2, 0, core),
    )
    goal_slot = jnp.where(
        carries_back, jnp.where(column == 0, 5, 7), jnp.where(column == 2, 0, 1)
    )
    twice = jnp.logical_or(column == 0, jnp.logical_and(column == 3, core == 1))
    goal_two = jnp.where(column == 0, plane - 4 + core, 2)
    goal_two_slot = jnp.where(column == 0, 7, 0)
    origin = jnp.where(
        carries_back,
        plane + 2 * column + core - here,
        -lanes + 2 * column + core - here,
    )

    def signal(offset):
        pl.semaphore_signal(
            barrier, inc=1, device_id=device(offset), device_id_type=MESH
        )

    barrier = pltpu.get_barrier_semaphore()
    senders = [k + p for p in (corpus, 0) for k in range(-4, 4) if k + p]
    for offset in senders:
        signal(offset)

    @pl.when(carries)
    def _():
        signal(origin)

    def greet_carriers(place, from_column, from_core):
        def body(p, carry):
            signal(p * lanes + 2 * from_column + from_core - place)
            return carry

        lax.fori_loop(0, PIECES, body, 0)

    @pl.when(high)
    def _():
        greet_carriers(here, 0, core)
        greet_carriers(here, 1, core)

    @pl.when(low)
    def _():
        greet_carriers(here, 3, core)

    @pl.when(here == 0)
    def _():
        greet_carriers(here, 2, 1)

    @pl.when(jnp.logical_and(here >= plane - 4, here < plane - 2))
    def _():
        greet_carriers(here, 0, core)

    @pl.when(here == 2)
    def _():
        greet_carriers(here, 3, 1)

    at_seam = jnp.logical_or(low, high)
    late_last = here >= plane - 4
    is_source = jnp.logical_or(back_source, ahead_source)
    pl.semaphore_wait(
        barrier,
        len(senders)
        + jnp.where(carries, 1, 0)
        + jnp.where(twice, 1, 0)
        + jnp.where(is_source, PIECES, 0),
    )

    z_fresh = pltpu.make_async_remote_copy(
        src_ref=fresh_ref,
        dst_ref=blocks.at[block(OWN), mine],
        send_sem=zf_send,
        recv_sem=zf_recv,
        device_id=partner,
        device_id_type=MESH,
    )
    z_fresh.start()

    def z_replay(step):
        at, size = chunks[step]
        return pltpu.make_async_remote_copy(
            src_ref=replay_ref.at[
                pl.ds(pl.multiple_of((1 - me_f) * share + at, size), size), :
            ],
            dst_ref=slab.at[pl.ds(at, size), mine],
            send_sem=zr_send.at[step],
            recv_sem=zr_recv.at[step],
            device_id=partner,
            device_id_type=MESH,
        )

    own_fresh = pltpu.make_async_copy(
        fresh_ref, blocks.at[block(OWN), mine], local_sem.at[0]
    )
    own_replay = pltpu.make_async_copy(
        replay_ref.at[pl.ds(pl.multiple_of(me_f * share, share), share), :],
        slab.at[:, mine],
        local_sem.at[1],
    )

    def spread(phase):
        cols = mine if phase == 0 else other
        source = fresh_ref if phase == 0 else blocks.at[block(OWN), cols]

        def to(index, target, slot):
            return pltpu.make_async_remote_copy(
                src_ref=source,
                dst_ref=blocks.at[block(slot), cols],
                send_sem=out_send.at[phase, index],
                recv_sem=block_recv.at[phase, slot],
                device_id=target,
                device_id_type=MESH,
            )

        return [
            (jnp.logical_not(low), to(0, device(-2), 5)),
            (jnp.logical_not(high), to(1, device(2), 1)),
            (None, to(2, twin, 2 + 2 * core)),
        ]

    def edge(p):
        at = pl.ds(pl.multiple_of(p * piece, piece), piece)
        return pltpu.make_async_remote_copy(
            src_ref=fresh_ref.at[at, :],
            dst_ref=carried.at[0],
            send_sem=edge_send.at[p],
            recv_sem=carry_recv.at[0],
            device_id=carrier(p),
            device_id_type=MESH,
        )

    swap = pltpu.make_async_remote_copy(
        src_ref=carried.at[0],
        dst_ref=carried.at[1],
        send_sem=swap_send,
        recv_sem=carry_recv.at[1],
        device_id=partner,
        device_id_type=MESH,
    )

    def feature_half(phase, offset):
        sender = device(offset)[1]
        return columns(sender if phase == 0 else 1 - sender)

    def hand_over(phase):
        def to(index, target, slot):
            at = pl.ds(pl.multiple_of(slot * rows + row * piece, piece), piece)
            return pltpu.make_async_remote_copy(
                src_ref=carried.at[phase],
                dst_ref=blocks.at[at, feature_half(phase, origin)],
                send_sem=carry_send.at[phase, index],
                recv_sem=block_recv.at[phase, slot],
                device_id=device(target - here),
                device_id_type=MESH,
            )

        return [
            (carries, to(0, goal, goal_slot)),
            (twice, to(1, goal_two, goal_two_slot)),
        ]

    def passing(phase, slot):
        cols = feature_half(phase, slot - BEHIND)

        def to(index, target, there):
            return pltpu.make_async_remote_copy(
                src_ref=blocks.at[block(slot), cols],
                dst_ref=blocks.at[block(there), cols],
                send_sem=pass_send.at[phase, index],
                recv_sem=block_recv.at[phase, there],
                device_id=target,
                device_id_type=MESH,
            )

        if slot == 1:
            onward = jnp.logical_and(core == 1, jnp.logical_not(at_seam))
            return [
                (onward, to(0, device(1), 0)),
                (None, to(1, twin, 2 * core)),
            ]
        if slot == 5:
            return [
                (jnp.logical_not(at_seam), to(2, device(-2), 7)),
                (None, to(3, twin, 4 + 2 * core)),
            ]
        return [(core == 0, to(4, twin, 6))]

    def each(pairs, act):
        for condition, copy in pairs:
            if condition is None:
                act(copy)
            else:
                pl.when(condition)(functools.partial(act, copy))

    def start(copy):
        copy.start()

    def sent(copy):
        copy.wait_send()

    def arrival(phase, slot):
        pltpu.make_async_copy(
            blocks.at[block(slot), mine],
            blocks.at[block(slot), mine],
            block_recv.at[phase, slot],
        ).wait()

    def start_edge():
        @pl.when(is_source)
        def _():
            def body(p, carry):
                edge(p).start()
                return carry

            lax.fori_loop(0, PIECES, body, 0)

    def pass_on(phase, slot):
        arrival(phase, slot)
        each(passing(phase, slot), start)

    def finish_spread(phase):
        each(spread(phase), sent)
        for slot in (1, 5, 7):
            each(passing(phase, slot), sent)
        each(hand_over(phase), sent)

    def finish_edge():
        @pl.when(is_source)
        def _():
            def body(p, carry):
                edge(p).wait_send()
                return carry

            lax.fori_loop(0, PIECES, body, 0)

        @pl.when(carries)
        def _():
            swap.wait_send()

    start_edge()
    each(spread(0), start)
    own_fresh.start()
    own_replay.start()

    fresh_max[...] = jnp.full_like(fresh_max, NEG_FLOOR)
    fresh_sum[...] = jnp.zeros_like(fresh_sum)
    stats[...] = jnp.zeros_like(stats)

    @pl.when(carries)
    def _():
        pltpu.make_async_copy(carried.at[0], carried.at[0], carry_recv.at[0]).wait()
        swap.start()

    each(hand_over(0), start)
    z_fresh.wait_send()
    for step in range(len(chunks)):
        z_replay(step).start()
    for slot in (1, 5):
        pass_on(0, slot)
    z_fresh.wait_recv()
    each(spread(1), start)

    @pl.when(carries)
    def _():
        swap.wait_recv()

    each(hand_over(1), start)
    pass_on(0, 7)

    @pl.when(jnp.logical_not(at_seam))
    def _():
        for slot in (1, 5):
            pass_on(1, slot)

    @pl.when(jnp.logical_not(late_last))
    def _():
        pass_on(1, 7)

    own_fresh.wait()
    own_replay.wait()

    def score_block(at, size, slot):
        block_rows = block(slot)
        score = (
            lax.dot_general(
                slab[at : at + size, :],
                blocks[block_rows, :],
                (((1,), (1,)), ((), ())),
                preferred_element_type=jnp.float32,
            )
            * scale
        )
        scores[slot, :size, :] = score
        grouped = score.reshape(size // 8, 8, rows)
        old = fresh_max[slot]
        new = jnp.maximum(old, jnp.max(grouped, axis=0))
        fresh_max[slot] = new
        fresh_sum[slot] = fresh_sum[slot] * jnp.exp2(old - new) + jnp.sum(
            jnp.exp2(grouped - new[None]), axis=0
        )

    def finish_rows(at, start_row, size):
        tiles = [
            scores[k, start_row : start_row + size, j : j + 128]
            for k in range(WINDOW)
            for j in range(0, rows, 128)
        ]
        row_max = functools.reduce(jnp.maximum, tiles)
        row_sum = functools.reduce(
            jnp.add, [jnp.exp2(tile - row_max) for tile in tiles]
        )
        row_max = row_max.T
        row_sum = row_sum.T
        top = jnp.max(row_max, axis=0, keepdims=True)
        total = jnp.sum(row_sum * jnp.exp2(row_max - top), axis=0, keepdims=True)
        first = at // 128
        replay_out[first : first + 1, :] = LN2 * (top + jnp.log2(total))

    first_rows = sum(size for _, size in chunks[:first_steps])
    for step in range(first_steps):
        z_replay(step).wait_recv()

    def visit_block(index, carry):
        slot = jnp.where(here < plane // 2, WINDOW - 1 - index, index)

        @pl.when(lax.rem(slot, 2) == 0)
        def _():
            for phase in (0, 1):
                arrival(phase, slot)

        for late, there in ((at_seam, 1), (at_seam, 5), (late_last, 7)):

            @pl.when(jnp.logical_and(late, slot == there))
            def _(there=there):
                pass_on(1, there)

        score_block(0, first_rows, slot)
        return carry

    lax.fori_loop(0, WINDOW, visit_block, 0)
    for at in range(0, first_rows, 128):
        finish_rows(at, at, 128)

    for step in range(first_steps, len(chunks)):
        at, size = chunks[step]
        z_replay(step).wait_recv()
        for slot in range(WINDOW):
            score_block(at, size, slot)
        for start_row in range(0, size, 128):
            finish_rows(at + start_row, start_row, 128)

    for k in range(WINDOW):
        top = jnp.max(fresh_max[k], axis=0, keepdims=True)
        total = jnp.sum(
            fresh_sum[k] * jnp.exp2(fresh_max[k] - top), axis=0, keepdims=True
        )
        for j in range(rows // 128):
            stats[k, j : j + 1, :] = top[:, j * 128 : (j + 1) * 128]
            stats[k, 2 + j : 3 + j, :] = total[:, j * 128 : (j + 1) * 128]

    def send_stats(k, side):
        return pltpu.make_async_remote_copy(
            src_ref=stats.at[k],
            dst_ref=landed.at[side, k],
            send_sem=stat_send.at[side, k],
            recv_sem=stat_recv.at[side, k],
            device_id=device(k - BEHIND + side * corpus),
            device_id_type=MESH,
        )

    outward = [
        (k, side) for side in (1, 0) for k in range(WINDOW) if side or k != BEHIND
    ]
    for k, side in outward:
        send_stats(k, side).start()
    landed[0, BEHIND] = stats[BEHIND]
    finish_edge()
    for phase in (0, 1):
        finish_spread(phase)
    for step in range(len(chunks)):
        z_replay(step).wait_send()
    for k, side in outward:
        send_stats(k, side).wait()
    got = landed[...].reshape(2 * WINDOW, 8, 128)
    top = jnp.max(got[:, 0:2, :], axis=0)
    total = jnp.sum(got[:, 2:4, :] * jnp.exp2(got[:, 0:2, :] - top[None]), axis=0)
    fresh_out[...] = LN2 * (top + jnp.log2(total))


def per_device(corpus, plane, fresh_embed, replay_embed):
    rows, half = fresh_embed.shape
    share = replay_embed.shape[0] // 2
    sizes = (128, 128, 256, 256, 128, 128)
    chunks = [(sum(sizes[:i]), size) for i, size in enumerate(sizes)]
    first_steps = 3
    most = max(sum(sizes[:first_steps]), max(sizes))
    full = 2 * half
    scale = 0.25 / math.sqrt(full) * math.log2(math.e)
    dma = pltpu.SemaphoreType.DMA
    fresh_lse, replay_lse = pl.pallas_call(
        functools.partial(kernel, corpus, plane, chunks, first_steps, scale),
        out_shape=(
            jax.ShapeDtypeStruct((rows // 128, 128), jnp.float32),
            jax.ShapeDtypeStruct((share // 128, 128), jnp.float32),
        ),
        in_specs=[pl.BlockSpec(memory_space=pltpu.HBM)] * 2,
        out_specs=[pl.BlockSpec(memory_space=pltpu.VMEM)] * 2,
        scratch_shapes=[
            pltpu.VMEM((WINDOW * rows, full), jnp.bfloat16),
            pltpu.VMEM((share, full), jnp.bfloat16),
            pltpu.VMEM((WINDOW, most, rows), jnp.float32),
            pltpu.VMEM((WINDOW, 8, rows), jnp.float32),
            pltpu.VMEM((WINDOW, 8, rows), jnp.float32),
            pltpu.VMEM((WINDOW, 8, 128), jnp.float32),
            pltpu.VMEM((2, WINDOW, 8, 128), jnp.float32),
            pltpu.VMEM((2, rows // PIECES, half), jnp.bfloat16),
            dma((2,)),
            dma,
            dma,
            dma((len(chunks),)),
            dma((len(chunks),)),
            dma((2, 3)),
            dma((2, 5)),
            dma((PIECES,)),
            dma((2, WINDOW)),
            dma,
            dma((2, 2)),
            dma((2,)),
            dma((2, WINDOW)),
            dma((2, WINDOW)),
        ],
        compiler_params=pltpu.CompilerParams(
            collective_id=0, has_side_effects=True, vmem_limit_bytes=60 * 2**20
        ),
    )(fresh_embed, replay_embed)
    return fresh_lse.reshape(rows), replay_lse.reshape(share)


def solution(mesh):
    placed = (P("corpus", "feat"), P("corpus", "feat"))
    return jax.shard_map(
        functools.partial(per_device, mesh.shape["corpus"], PLANE),
        mesh=mesh,
        in_specs=placed,
        out_specs=(P("corpus"), P(("corpus", "feat"))),
        check_vma=False,
    )
```

```python
import functools
import math

import jax
import jax.numpy as jnp
from jax import lax
from jax.experimental import pallas as pl
from jax.experimental.pallas import tpu as pltpu
from jax.sharding import PartitionSpec as P

MESH = pl.DeviceIdType.MESH
WINDOW = 8
BEHIND = 3
OWN = 3
PLANE = 64
PIECES = 8
NEG_FLOOR = -1e30
LN2 = math.log(2.0)
PARTS = 2


def kernel(
    corpus,
    plane,
    chunks,
    first_steps,
    scale,
    fresh_ref,
    replay_ref,
    fresh_out,
    replay_out,
    blocks,
    slab,
    scores,
    fresh_max,
    fresh_sum,
    stats,
    landed,
    carried,
    local_sem,
    zf_send,
    zf_recv,
    zr_send,
    zr_recv,
    out_send,
    pass_send,
    edge_send,
    block_recv,
    swap_send,
    carry_send,
    carry_recv,
    stat_send,
    stat_recv,
):
    rows, half = fresh_ref.shape
    share = replay_ref.shape[0] // 2
    lanes = plane // PIECES
    piece = rows // PIECES
    me_c = lax.axis_index("corpus")
    me_f = lax.axis_index("feat")
    ring = 2 * corpus
    me = me_f * corpus + me_c
    here = lax.rem(me_c, plane)
    core = lax.rem(here, 2)
    column = lax.rem(here, lanes) // 2
    row = here // lanes

    def device(offset):
        there = lax.rem(me + offset + ring, ring)
        return (lax.rem(there, corpus), there // corpus)

    sub = rows // PARTS

    def block(slot, part=0):
        if part == 0:
            return pl.ds(pl.multiple_of(slot * rows, rows), rows)
        return pl.ds(pl.multiple_of(slot * rows + (part - 1) * sub, sub), sub)

    def columns(feature_half):
        return pl.ds(pl.multiple_of(feature_half * half, half), half)

    partner = device(corpus)
    twin = device(1 - 2 * core)
    mine = columns(me_f)
    other = columns(1 - me_f)
    low = here < 2
    high = here >= plane - 2
    back_source = here < 4
    ahead_source = here >= plane - 3
    carries_back = column < 2
    carries = jnp.logical_or(column != 2, core == 1)

    def carrier(p):
        there = p * lanes + 2 * column + core
        return device(there - here + jnp.where(back_source, -plane, plane))

    goal = jnp.where(
        carries_back,
        plane - 2 + core,
        jnp.where(column == 2, 0, core),
    )
    goal_slot = jnp.where(
        carries_back, jnp.where(column == 0, 5, 7), jnp.where(column == 2, 0, 1)
    )
    twice = jnp.logical_or(column == 0, jnp.logical_and(column == 3, core == 1))
    goal_two = jnp.where(column == 0, plane - 4 + core, 2)
    goal_two_slot = jnp.where(column == 0, 7, 0)
    origin = jnp.where(
        carries_back,
        plane + 2 * column + core - here,
        -lanes + 2 * column + core - here,
    )

    def signal(offset):
        pl.semaphore_signal(
            barrier, inc=1, device_id=device(offset), device_id_type=MESH
        )

    barrier = pltpu.get_barrier_semaphore()
    senders = [k + p for p in (corpus, 0) for k in range(-4, 4) if k + p]
    for offset in senders:
        signal(offset)

    @pl.when(carries)
    def _():
        signal(origin)

    def greet_carriers(place, from_column, from_core):
        def body(p, carry):
            signal(p * lanes + 2 * from_column + from_core - place)
            return carry

        lax.fori_loop(0, PIECES, body, 0)

    @pl.when(high)
    def _():
        greet_carriers(here, 0, core)
        greet_carriers(here, 1, core)

    @pl.when(low)
    def _():
        greet_carriers(here, 3, core)

    @pl.when(here == 0)
    def _():
        greet_carriers(here, 2, 1)

    @pl.when(jnp.logical_and(here >= plane - 4, here < plane - 2))
    def _():
        greet_carriers(here, 0, core)

    @pl.when(here == 2)
    def _():
        greet_carriers(here, 3, 1)

    at_seam = jnp.logical_or(low, high)
    is_source = jnp.logical_or(back_source, ahead_source)
    pl.semaphore_wait(
        barrier,
        len(senders)
        + jnp.where(carries, 1, 0)
        + jnp.where(twice, 1, 0)
        + jnp.where(is_source, PIECES, 0),
    )

    def z_fresh(part):
        return pltpu.make_async_remote_copy(
            src_ref=fresh_ref.at[pl.ds((part - 1) * sub, sub), :],
            dst_ref=blocks.at[block(OWN, part), mine],
            send_sem=zf_send.at[part - 1],
            recv_sem=zf_recv.at[part - 1],
            device_id=partner,
            device_id_type=MESH,
        )

    for part in range(1, PARTS + 1):
        z_fresh(part).start()

    def z_replay(step):
        at, size = chunks[step]
        return pltpu.make_async_remote_copy(
            src_ref=replay_ref.at[
                pl.ds(pl.multiple_of((1 - me_f) * share + at, size), size), :
            ],
            dst_ref=slab.at[pl.ds(at, size), mine],
            send_sem=zr_send.at[step],
            recv_sem=zr_recv.at[step],
            device_id=partner,
            device_id_type=MESH,
        )

    own_fresh = pltpu.make_async_copy(
        fresh_ref, blocks.at[block(OWN), mine], local_sem.at[0]
    )
    own_replay = pltpu.make_async_copy(
        replay_ref.at[pl.ds(pl.multiple_of(me_f * share, share), share), :],
        slab.at[:, mine],
        local_sem.at[1],
    )

    def spread(part):
        cols = mine if part == 0 else other
        source = fresh_ref if part == 0 else blocks.at[block(OWN, part), cols]

        def to(index, target, slot):
            return pltpu.make_async_remote_copy(
                src_ref=source,
                dst_ref=blocks.at[block(slot, part), cols],
                send_sem=out_send.at[part, index],
                recv_sem=block_recv.at[part, slot],
                device_id=target,
                device_id_type=MESH,
            )

        return [
            (jnp.logical_not(low), to(0, device(-2), 5)),
            (jnp.logical_not(high), to(1, device(2), 1)),
            (None, to(2, twin, 2 + 2 * core)),
        ]

    def edge(p):
        at = pl.ds(pl.multiple_of(p * piece, piece), piece)
        return pltpu.make_async_remote_copy(
            src_ref=fresh_ref.at[at, :],
            dst_ref=carried.at[0],
            send_sem=edge_send.at[p],
            recv_sem=carry_recv.at[0],
            device_id=carrier(p),
            device_id_type=MESH,
        )

    swap = pltpu.make_async_remote_copy(
        src_ref=carried.at[0],
        dst_ref=carried.at[1],
        send_sem=swap_send,
        recv_sem=carry_recv.at[1],
        device_id=partner,
        device_id_type=MESH,
    )

    def feature_half(phase, offset):
        sender = device(offset)[1]
        return columns(sender if phase == 0 else 1 - sender)

    def hand_over(phase):
        def to(index, target, slot):
            at = pl.ds(pl.multiple_of(slot * rows + row * piece, piece), piece)
            return pltpu.make_async_remote_copy(
                src_ref=carried.at[phase],
                dst_ref=blocks.at[at, feature_half(phase, origin)],
                send_sem=carry_send.at[phase, index],
                recv_sem=block_recv.at[
                    0 if phase == 0 else 1 + row * PARTS // PIECES, slot
                ],
                device_id=device(target - here),
                device_id_type=MESH,
            )

        return [
            (carries, to(0, goal, goal_slot)),
            (twice, to(1, goal_two, goal_two_slot)),
        ]

    def passing(part, slot):
        cols = feature_half(min(part, 1), slot - BEHIND)

        def to(index, target, there):
            return pltpu.make_async_remote_copy(
                src_ref=blocks.at[block(slot, part), cols],
                dst_ref=blocks.at[block(there, part), cols],
                send_sem=pass_send.at[part, index],
                recv_sem=block_recv.at[part, there],
                device_id=target,
                device_id_type=MESH,
            )

        if slot == 1:
            onward = jnp.logical_and(core == 1, jnp.logical_not(at_seam))
            return [
                (onward, to(0, device(1), 0)),
                (None, to(1, twin, 2 * core)),
            ]
        if slot == 5:
            return [
                (jnp.logical_not(at_seam), to(2, device(-2), 7)),
                (None, to(3, twin, 4 + 2 * core)),
            ]
        return [(core == 0, to(4, twin, 6))]

    def each(pairs, act):
        for condition, copy in pairs:
            if condition is None:
                act(copy)
            else:
                pl.when(condition)(functools.partial(act, copy))

    def start(copy):
        copy.start()

    def sent(copy):
        copy.wait_send()

    def arrival(part, slot):
        pltpu.make_async_copy(
            blocks.at[block(slot, part), mine],
            blocks.at[block(slot, part), mine],
            block_recv.at[part, slot],
        ).wait()

    def start_edge():
        @pl.when(is_source)
        def _():
            def body(p, carry):
                edge(p).start()
                return carry

            lax.fori_loop(0, PIECES, body, 0)

    def pass_on(part, slot):
        arrival(part, slot)
        each(passing(part, slot), start)

    later = range(1, PARTS + 1)

    def finish_edge():
        @pl.when(is_source)
        def _():
            def body(p, carry):
                edge(p).wait_send()
                return carry

            lax.fori_loop(0, PIECES, body, 0)

        @pl.when(carries)
        def _():
            swap.wait_send()

    start_edge()
    each(spread(0), start)
    own_fresh.start()
    own_replay.start()

    fresh_max[...] = jnp.full_like(fresh_max, NEG_FLOOR)
    fresh_sum[...] = jnp.zeros_like(fresh_sum)
    stats[...] = jnp.zeros_like(stats)

    @pl.when(carries)
    def _():
        pltpu.make_async_copy(carried.at[0], carried.at[0], carry_recv.at[0]).wait()
        swap.start()

    each(hand_over(0), start)
    for part in later:
        z_fresh(part).wait_send()
    z_replay(0).start()
    for slot in (1, 5):
        pass_on(0, slot)
    for part in later:
        z_fresh(part).wait_recv()
        each(spread(part), start)
    for step in range(1, len(chunks)):
        z_replay(step).start()

    @pl.when(carries)
    def _():
        swap.wait_recv()

    each(hand_over(1), start)
    pass_on(0, 7)

    for part in later:
        for slot in (1, 5):
            pass_on(part, slot)
    for part in later:
        pass_on(part, 7)

    own_fresh.wait()
    own_replay.wait()

    def score_block(at, size, slot):
        block_rows = block(slot)
        score = (
            lax.dot_general(
                slab[at : at + size, :],
                blocks[block_rows, :],
                (((1,), (1,)), ((), ())),
                preferred_element_type=jnp.float32,
            )
            * scale
        )
        scores[slot, :size, :] = score
        grouped = score.reshape(size // 8, 8, rows)
        old = fresh_max[slot]
        new = jnp.maximum(old, jnp.max(grouped, axis=0))
        fresh_max[slot] = new
        fresh_sum[slot] = fresh_sum[slot] * jnp.exp2(old - new) + jnp.sum(
            jnp.exp2(grouped - new[None]), axis=0
        )

    def finish_rows(at, start_row, size):
        tiles = [
            scores[k, start_row : start_row + size, j : j + 128]
            for k in range(WINDOW)
            for j in range(0, rows, 128)
        ]
        row_max = functools.reduce(jnp.maximum, tiles)
        row_sum = functools.reduce(
            jnp.add, [jnp.exp2(tile - row_max) for tile in tiles]
        )
        row_max = row_max.T
        row_sum = row_sum.T
        top = jnp.max(row_max, axis=0, keepdims=True)
        total = jnp.sum(row_sum * jnp.exp2(row_max - top), axis=0, keepdims=True)
        first = at // 128
        replay_out[first : first + 1, :] = LN2 * (top + jnp.log2(total))

    first_rows = sum(size for _, size in chunks[:first_steps])
    for step in range(first_steps):
        z_replay(step).wait_recv()

    def visit_block(index, carry):
        slot = jnp.where(here < plane // 2, WINDOW - 1 - index, index)

        @pl.when(lax.rem(slot, 2) == 0)
        def _():
            for part in range(PARTS + 1):
                arrival(part, slot)

        score_block(0, first_rows, slot)
        return carry

    lax.fori_loop(0, WINDOW, visit_block, 0)
    for at in range(0, first_rows, 128):
        finish_rows(at, at, 128)

    for step in range(first_steps, len(chunks)):
        at, size = chunks[step]
        z_replay(step).wait_recv()
        for slot in range(WINDOW):
            score_block(at, size, slot)
        for start_row in range(0, size, 128):
            finish_rows(at + start_row, start_row, 128)

    for k in range(WINDOW):
        top = jnp.max(fresh_max[k], axis=0, keepdims=True)
        total = jnp.sum(
            fresh_sum[k] * jnp.exp2(fresh_max[k] - top), axis=0, keepdims=True
        )
        for j in range(rows // 128):
            stats[k, j : j + 1, :] = top[:, j * 128 : (j + 1) * 128]
            stats[k, 2 + j : 3 + j, :] = total[:, j * 128 : (j + 1) * 128]

    def send_stats(k, side):
        return pltpu.make_async_remote_copy(
            src_ref=stats.at[k],
            dst_ref=landed.at[side, k],
            send_sem=stat_send.at[side, k],
            recv_sem=stat_recv.at[side, k],
            device_id=device(k - BEHIND + side * corpus),
            device_id_type=MESH,
        )

    outward = [
        (k, side) for side in (1, 0) for k in range(WINDOW) if side or k != BEHIND
    ]
    for k, side in outward:
        send_stats(k, side).start()
    landed[0, BEHIND] = stats[BEHIND]
    finish_edge()
    for phase in (0, 1):
        each(hand_over(phase), sent)
    for part in range(PARTS + 1):
        each(spread(part), sent)
        for slot in (1, 5, 7):
            each(passing(part, slot), sent)
    for step in range(len(chunks)):
        z_replay(step).wait_send()
    for k, side in outward:
        send_stats(k, side).wait()
    got = landed[...].reshape(2 * WINDOW, 8, 128)
    top = jnp.max(got[:, 0:2, :], axis=0)
    total = jnp.sum(got[:, 2:4, :] * jnp.exp2(got[:, 0:2, :] - top[None]), axis=0)
    fresh_out[...] = LN2 * (top + jnp.log2(total))


def per_device(corpus, plane, fresh_embed, replay_embed):
    rows, half = fresh_embed.shape
    share = replay_embed.shape[0] // 2
    sizes = (128, 128, 256, 256, 128, 128)
    chunks = [(sum(sizes[:i]), size) for i, size in enumerate(sizes)]
    first_steps = 3
    most = max(sum(sizes[:first_steps]), max(sizes))
    full = 2 * half
    scale = 0.25 / math.sqrt(full) * math.log2(math.e)
    dma = pltpu.SemaphoreType.DMA
    fresh_lse, replay_lse = pl.pallas_call(
        functools.partial(kernel, corpus, plane, chunks, first_steps, scale),
        out_shape=(
            jax.ShapeDtypeStruct((rows // 128, 128), jnp.float32),
            jax.ShapeDtypeStruct((share // 128, 128), jnp.float32),
        ),
        in_specs=[pl.BlockSpec(memory_space=pltpu.HBM)] * 2,
        out_specs=[pl.BlockSpec(memory_space=pltpu.VMEM)] * 2,
        scratch_shapes=[
            pltpu.VMEM((WINDOW * rows, full), jnp.bfloat16),
            pltpu.VMEM((share, full), jnp.bfloat16),
            pltpu.VMEM((WINDOW, most, rows), jnp.float32),
            pltpu.VMEM((WINDOW, 8, rows), jnp.float32),
            pltpu.VMEM((WINDOW, 8, rows), jnp.float32),
            pltpu.VMEM((WINDOW, 8, 128), jnp.float32),
            pltpu.VMEM((2, WINDOW, 8, 128), jnp.float32),
            pltpu.VMEM((2, rows // PIECES, half), jnp.bfloat16),
            dma((2,)),
            dma((PARTS,)),
            dma((PARTS,)),
            dma((len(chunks),)),
            dma((len(chunks),)),
            dma((PARTS + 1, 3)),
            dma((PARTS + 1, 5)),
            dma((PIECES,)),
            dma((PARTS + 1, WINDOW)),
            dma,
            dma((2, 2)),
            dma((2,)),
            dma((2, WINDOW)),
            dma((2, WINDOW)),
        ],
        compiler_params=pltpu.CompilerParams(
            collective_id=0, has_side_effects=True, vmem_limit_bytes=60 * 2**20
        ),
    )(fresh_embed, replay_embed)
    return fresh_lse.reshape(rows), replay_lse.reshape(share)


def solution(mesh):
    placed = (P("corpus", "feat"), P("corpus", "feat"))
    return jax.shard_map(
        functools.partial(per_device, mesh.shape["corpus"], PLANE),
        mesh=mesh,
        in_specs=placed,
        out_specs=(P("corpus"), P(("corpus", "feat"))),
        check_vma=False,
    )
```

```python
import functools
import math

import jax
import jax.numpy as jnp
from jax import lax
from jax.experimental import pallas as pl
from jax.experimental.pallas import tpu as pltpu
from jax.sharding import PartitionSpec as P

MESH = pl.DeviceIdType.MESH
WINDOW = 8
BEHIND = 3
OWN = 3
PLANE = 64
PIECES = 8
NEG_FLOOR = -1e30
LN2 = math.log(2.0)
VMEM_BYTES = 55104 * 1024
PARTS = 2


def kernel(
    corpus,
    plane,
    chunks,
    first_steps,
    scale,
    fresh_ref,
    replay_ref,
    fresh_out,
    replay_out,
    blocks,
    slab,
    scores,
    fresh_max,
    fresh_sum,
    stats,
    landed,
    carried,
    local_sem,
    zf_send,
    zf_recv,
    zr_send,
    zr_recv,
    out_send,
    pass_send,
    edge_send,
    block_recv,
    swap_send,
    carry_send,
    carry_recv,
    stat_send,
    stat_recv,
):
    rows, half = fresh_ref.shape
    share = replay_ref.shape[0] // 2
    lanes = plane // PIECES
    piece = rows // PIECES
    me_c = lax.axis_index("corpus")
    me_f = lax.axis_index("feat")
    ring = 2 * corpus
    me = me_f * corpus + me_c
    here = lax.rem(me_c, plane)
    core = lax.rem(here, 2)
    column = lax.rem(here, lanes) // 2
    row = here // lanes

    def device(offset):
        there = lax.rem(me + offset + ring, ring)
        return (lax.rem(there, corpus), there // corpus)

    sub = rows // PARTS

    def block(slot, part=0):
        if part == 0:
            return pl.ds(pl.multiple_of(slot * rows, rows), rows)
        return pl.ds(pl.multiple_of(slot * rows + (part - 1) * sub, sub), sub)

    def columns(feature_half):
        return pl.ds(pl.multiple_of(feature_half * half, half), half)

    partner = device(corpus)
    twin = device(1 - 2 * core)
    mine = columns(me_f)
    other = columns(1 - me_f)
    low = here < 2
    high = here >= plane - 2
    back_source = here < 4
    ahead_source = here >= plane - 3
    carries_back = column < 2
    carries = jnp.logical_or(column != 2, core == 1)

    def carrier(p):
        there = p * lanes + 2 * column + core
        return device(there - here + jnp.where(back_source, -plane, plane))

    goal = jnp.where(
        carries_back,
        plane - 2 + core,
        jnp.where(column == 2, 0, core),
    )
    goal_slot = jnp.where(
        carries_back, jnp.where(column == 0, 5, 7), jnp.where(column == 2, 0, 1)
    )
    twice = jnp.logical_or(column == 0, jnp.logical_and(column == 3, core == 1))
    goal_two = jnp.where(column == 0, plane - 4 + core, 2)
    goal_two_slot = jnp.where(column == 0, 7, 0)
    origin = jnp.where(
        carries_back,
        plane + 2 * column + core - here,
        -lanes + 2 * column + core - here,
    )

    def signal(offset):
        pl.semaphore_signal(
            barrier, inc=1, device_id=device(offset), device_id_type=MESH
        )

    barrier = pltpu.get_barrier_semaphore()
    senders = [corpus] + [k + p for p in (corpus, 0) for k in range(-4, 4) if k]
    for offset in senders:
        signal(offset)

    @pl.when(carries)
    def _():
        signal(origin)

    def greet_carriers(place, from_column, from_core):
        def body(p, carry):
            signal(p * lanes + 2 * from_column + from_core - place)
            return carry

        lax.fori_loop(0, PIECES, body, 0)

    @pl.when(high)
    def _():
        greet_carriers(here, 0, core)
        greet_carriers(here, 1, core)

    @pl.when(low)
    def _():
        greet_carriers(here, 3, core)

    @pl.when(here == 0)
    def _():
        greet_carriers(here, 2, 1)

    @pl.when(jnp.logical_and(here >= plane - 4, here < plane - 2))
    def _():
        greet_carriers(here, 0, core)

    @pl.when(here == 2)
    def _():
        greet_carriers(here, 3, 1)

    at_seam = jnp.logical_or(low, high)
    is_source = jnp.logical_or(back_source, ahead_source)
    pl.semaphore_wait(
        barrier,
        len(senders)
        + jnp.where(carries, 1, 0)
        + jnp.where(twice, 1, 0)
        + jnp.where(is_source, PIECES, 0),
    )

    def z_fresh(part):
        return pltpu.make_async_remote_copy(
            src_ref=fresh_ref.at[pl.ds((part - 1) * sub, sub), :],
            dst_ref=blocks.at[block(OWN, part), mine],
            send_sem=zf_send.at[part - 1],
            recv_sem=zf_recv.at[part - 1],
            device_id=partner,
            device_id_type=MESH,
        )


    def z_replay(step):
        at, size = chunks[step]
        return pltpu.make_async_remote_copy(
            src_ref=replay_ref.at[
                pl.ds(pl.multiple_of((1 - me_f) * share + at, size), size), :
            ],
            dst_ref=slab.at[pl.ds(at, size), mine],
            send_sem=zr_send.at[step],
            recv_sem=zr_recv.at[step],
            device_id=partner,
            device_id_type=MESH,
        )

    own_fresh = pltpu.make_async_copy(
        fresh_ref, blocks.at[block(OWN), mine], local_sem.at[0]
    )
    own_replay = pltpu.make_async_copy(
        replay_ref.at[pl.ds(pl.multiple_of(me_f * share, share), share), :],
        slab.at[:, mine],
        local_sem.at[1],
    )

    def spread(part):
        cols = mine if part == 0 else other
        source = fresh_ref if part == 0 else blocks.at[block(OWN, part), cols]

        def to(index, target, slot):
            return pltpu.make_async_remote_copy(
                src_ref=source,
                dst_ref=blocks.at[block(slot, part), cols],
                send_sem=out_send.at[part, index],
                recv_sem=block_recv.at[part, slot],
                device_id=target,
                device_id_type=MESH,
            )

        return [
            (jnp.logical_not(low), to(0, device(-2), 5)),
            (jnp.logical_not(high), to(1, device(2), 1)),
            (None, to(2, twin, 2 + 2 * core)),
        ]

    def edge(p):
        at = pl.ds(pl.multiple_of(p * piece, piece), piece)
        return pltpu.make_async_remote_copy(
            src_ref=fresh_ref.at[at, :],
            dst_ref=carried.at[0],
            send_sem=edge_send.at[p],
            recv_sem=carry_recv.at[0],
            device_id=carrier(p),
            device_id_type=MESH,
        )

    swap = pltpu.make_async_remote_copy(
        src_ref=carried.at[0],
        dst_ref=carried.at[1],
        send_sem=swap_send,
        recv_sem=carry_recv.at[1],
        device_id=partner,
        device_id_type=MESH,
    )

    def feature_half(phase, offset):
        sender = device(offset)[1]
        return columns(sender if phase == 0 else 1 - sender)

    def hand_over(phase):
        def to(index, target, slot):
            at = pl.ds(pl.multiple_of(slot * rows + row * piece, piece), piece)
            return pltpu.make_async_remote_copy(
                src_ref=carried.at[phase],
                dst_ref=blocks.at[at, feature_half(phase, origin)],
                send_sem=carry_send.at[phase, index],
                recv_sem=block_recv.at[
                    0 if phase == 0 else 1 + row * PARTS // PIECES, slot
                ],
                device_id=device(target - here),
                device_id_type=MESH,
            )

        return [
            (carries, to(0, goal, goal_slot)),
            (twice, to(1, goal_two, goal_two_slot)),
        ]

    def passing(part, slot):
        cols = feature_half(min(part, 1), slot - BEHIND)

        def to(index, target, there):
            return pltpu.make_async_remote_copy(
                src_ref=blocks.at[block(slot, part), cols],
                dst_ref=blocks.at[block(there, part), cols],
                send_sem=pass_send.at[part, index],
                recv_sem=block_recv.at[part, there],
                device_id=target,
                device_id_type=MESH,
            )

        if slot == 1:
            onward = jnp.logical_and(core == 1, jnp.logical_not(at_seam))
            return [
                (onward, to(0, device(1), 0)),
                (None, to(1, twin, 2 * core)),
            ]
        if slot == 5:
            return [
                (jnp.logical_not(at_seam), to(2, device(-2), 7)),
                (None, to(3, twin, 4 + 2 * core)),
            ]
        return [(core == 0, to(4, twin, 6))]

    def each(pairs, act):
        for condition, copy in pairs:
            if condition is None:
                act(copy)
            else:
                pl.when(condition)(functools.partial(act, copy))

    def start(copy):
        copy.start()

    def sent(copy):
        copy.wait_send()

    def arrival(part, slot):
        pltpu.make_async_copy(
            blocks.at[block(slot, part), mine],
            blocks.at[block(slot, part), mine],
            block_recv.at[part, slot],
        ).wait()

    def start_edge():
        @pl.when(is_source)
        def _():
            def body(p, carry):
                edge(p).start()
                return carry

            lax.fori_loop(0, PIECES, body, 0)

    def pass_on(part, slot):
        arrival(part, slot)
        each(passing(part, slot), start)

    later = range(1, PARTS + 1)

    def finish_edge():
        @pl.when(is_source)
        def _():
            def body(p, carry):
                edge(p).wait_send()
                return carry

            lax.fori_loop(0, PIECES, body, 0)

        @pl.when(carries)
        def _():
            swap.wait_send()

    z_fresh(1).start()
    start_edge()
    for part in later[1:]:
        z_fresh(part).start()
    each(spread(0), start)
    own_fresh.start()
    own_replay.start()

    fresh_max[...] = jnp.full_like(fresh_max, NEG_FLOOR)
    fresh_sum[...] = jnp.zeros_like(fresh_sum)
    stats[...] = jnp.zeros_like(stats)

    @pl.when(carries)
    def _():
        pltpu.make_async_copy(carried.at[0], carried.at[0], carry_recv.at[0]).wait()
        swap.start()

    each(hand_over(0), start)
    for part in later:
        z_fresh(part).wait_send()
    z_replay(0).start()
    for slot in (1, 5):
        pass_on(0, slot)
    for part in later:
        z_fresh(part).wait_recv()
        each(spread(part), start)
    for step in range(1, len(chunks)):
        z_replay(step).start()

    @pl.when(carries)
    def _():
        swap.wait_recv()

    each(hand_over(1), start)
    pass_on(0, 7)

    for part in later:
        for slot in (1, 5):
            pass_on(part, slot)
    for part in later:
        pass_on(part, 7)

    own_fresh.wait()
    own_replay.wait()

    def score_block(at, size, slot):
        block_rows = block(slot)
        score = (
            lax.dot_general(
                slab[at : at + size, :],
                blocks[block_rows, :],
                (((1,), (1,)), ((), ())),
                preferred_element_type=jnp.float32,
            )
            * scale
        )
        scores[slot, :size, :] = score
        grouped = score.reshape(size // 8, 8, rows)
        old = fresh_max[slot]
        new = jnp.maximum(old, jnp.max(grouped, axis=0))
        fresh_max[slot] = new
        fresh_sum[slot] = fresh_sum[slot] * jnp.exp2(old - new) + jnp.sum(
            jnp.exp2(grouped - new[None]), axis=0
        )

    def finish_rows(at, start_row, size):
        tiles = [
            scores[k, start_row : start_row + size, j : j + 128]
            for k in range(WINDOW)
            for j in range(0, rows, 128)
        ]
        row_max = functools.reduce(jnp.maximum, tiles)
        row_sum = functools.reduce(
            jnp.add, [jnp.exp2(tile - row_max) for tile in tiles]
        )
        row_max = row_max.T
        row_sum = row_sum.T
        top = jnp.max(row_max, axis=0, keepdims=True)
        total = jnp.sum(row_sum * jnp.exp2(row_max - top), axis=0, keepdims=True)
        first = at // 128
        replay_out[first : first + 1, :] = LN2 * (top + jnp.log2(total))

    first_rows = sum(size for _, size in chunks[:first_steps])
    for step in range(first_steps):
        z_replay(step).wait_recv()

    def visit_block(index, carry):
        slot = jnp.where(here < plane // 2, WINDOW - 1 - index, index)

        @pl.when(lax.rem(slot, 2) == 0)
        def _():
            for part in range(PARTS + 1):
                arrival(part, slot)

        score_block(0, first_rows, slot)
        return carry

    lax.fori_loop(0, WINDOW, visit_block, 0)
    for at in range(0, first_rows, 128):
        finish_rows(at, at, 128)

    for step in range(first_steps, len(chunks)):
        at, size = chunks[step]
        z_replay(step).wait_recv()
        for slot in range(WINDOW):
            score_block(at, size, slot)
        if step < len(chunks) - 1:
            for start_row in range(0, size, 128):
                finish_rows(at + start_row, start_row, 128)

    for k in range(WINDOW):
        top = jnp.max(fresh_max[k], axis=0, keepdims=True)
        total = jnp.sum(
            fresh_sum[k] * jnp.exp2(fresh_max[k] - top), axis=0, keepdims=True
        )
        for j in range(rows // 128):
            stats[k, j : j + 1, :] = top[:, j * 128 : (j + 1) * 128]
            stats[k, 2 + j : 3 + j, :] = total[:, j * 128 : (j + 1) * 128]

    def send_stats(k, side):
        return pltpu.make_async_remote_copy(
            src_ref=stats.at[k],
            dst_ref=landed.at[side, k],
            send_sem=stat_send.at[side, k],
            recv_sem=stat_recv.at[side, k],
            device_id=device(k - BEHIND + side * corpus),
            device_id_type=MESH,
        )

    outward = [
        (k, side) for side in (1, 0) for k in range(WINDOW) if side or k != BEHIND
    ]
    for k, side in outward:
        send_stats(k, side).start()
    landed[0, BEHIND] = stats[BEHIND]
    at, size = chunks[-1]
    for start_row in range(0, size, 128):
        finish_rows(at + start_row, start_row, 128)
    finish_edge()
    for phase in (0, 1):
        each(hand_over(phase), sent)
    for part in range(PARTS + 1):
        each(spread(part), sent)
        for slot in (1, 5, 7):
            each(passing(part, slot), sent)
    for step in range(len(chunks)):
        z_replay(step).wait_send()
    for k, side in outward:
        send_stats(k, side).wait()
    got = landed[...].reshape(2 * WINDOW, 8, 128)
    top = jnp.max(got[:, 0:2, :], axis=0)
    total = jnp.sum(got[:, 2:4, :] * jnp.exp2(got[:, 0:2, :] - top[None]), axis=0)
    fresh_out[...] = LN2 * (top + jnp.log2(total))


def per_device(corpus, plane, fresh_embed, replay_embed):
    rows, half = fresh_embed.shape
    share = replay_embed.shape[0] // 2
    sizes = (128, 128, 256, 256, 128, 128)
    chunks = [(sum(sizes[:i]), size) for i, size in enumerate(sizes)]
    first_steps = 3
    most = max(sum(sizes[:first_steps]), max(sizes))
    full = 2 * half
    scale = 0.25 / math.sqrt(full) * math.log2(math.e)
    dma = pltpu.SemaphoreType.DMA
    fresh_lse, replay_lse = pl.pallas_call(
        functools.partial(kernel, corpus, plane, chunks, first_steps, scale),
        out_shape=(
            jax.ShapeDtypeStruct((rows // 128, 128), jnp.float32),
            jax.ShapeDtypeStruct((share // 128, 128), jnp.float32),
        ),
        in_specs=[pl.BlockSpec(memory_space=pltpu.HBM)] * 2,
        out_specs=[pl.BlockSpec(memory_space=pltpu.VMEM)] * 2,
        scratch_shapes=[
            pltpu.VMEM((WINDOW * rows, full), jnp.bfloat16),
            pltpu.VMEM((share, full), jnp.bfloat16),
            pltpu.VMEM((WINDOW, most, rows), jnp.float32),
            pltpu.VMEM((WINDOW, 8, rows), jnp.float32),
            pltpu.VMEM((WINDOW, 8, rows), jnp.float32),
            pltpu.VMEM((WINDOW, 8, 128), jnp.float32),
            pltpu.VMEM((2, WINDOW, 8, 128), jnp.float32),
            pltpu.VMEM((2, rows // PIECES, half), jnp.bfloat16),
            dma((2,)),
            dma((PARTS,)),
            dma((PARTS,)),
            dma((len(chunks),)),
            dma((len(chunks),)),
            dma((PARTS + 1, 3)),
            dma((PARTS + 1, 5)),
            dma((PIECES,)),
            dma((PARTS + 1, WINDOW)),
            dma,
            dma((2, 2)),
            dma((2,)),
            dma((2, WINDOW)),
            dma((2, WINDOW)),
        ],
        compiler_params=pltpu.CompilerParams(
            collective_id=0, has_side_effects=True, vmem_limit_bytes=VMEM_BYTES
        ),
    )(fresh_embed, replay_embed)
    return fresh_lse.reshape(rows), replay_lse.reshape(share)


def solution(mesh):
    placed = (P("corpus", "feat"), P("corpus", "feat"))
    return jax.shard_map(
        functools.partial(per_device, mesh.shape["corpus"], PLANE),
        mesh=mesh,
        in_specs=placed,
        out_specs=(P("corpus"), P(("corpus", "feat"))),
        check_vma=False,
    )
```

```python
import functools
import math

import jax
import jax.numpy as jnp
from jax import lax
from jax.experimental import pallas as pl
from jax.experimental.pallas import tpu as pltpu
from jax.sharding import PartitionSpec as P

MESH = pl.DeviceIdType.MESH
WINDOW = 8
BEHIND = 3
OWN = 3
PLANE = 64
PIECES = 8
NEG_FLOOR = -1e30
LN2 = math.log(2.0)
VMEM_BYTES = 55104 * 1024
PARTS = 2


def kernel(
    corpus,
    plane,
    chunks,
    first_steps,
    scale,
    fresh_ref,
    replay_ref,
    fresh_out,
    replay_out,
    blocks,
    slab,
    scores,
    fresh_max,
    fresh_sum,
    stats,
    landed,
    carried,
    local_sem,
    zf_send,
    zf_recv,
    zr_send,
    zr_recv,
    out_send,
    pass_send,
    edge_send,
    block_recv,
    swap_send,
    carry_send,
    carry_recv,
    stat_send,
    stat_recv,
):
    rows, half = fresh_ref.shape
    share = replay_ref.shape[0] // 2
    lanes = plane // PIECES
    piece = rows // PIECES
    me_c = lax.axis_index("corpus")
    me_f = lax.axis_index("feat")
    ring = 2 * corpus
    me = me_f * corpus + me_c
    here = lax.rem(me_c, plane)
    core = lax.rem(here, 2)
    column = lax.rem(here, lanes) // 2
    row = here // lanes

    def device(offset):
        there = lax.rem(me + offset + ring, ring)
        return (lax.rem(there, corpus), there // corpus)

    sub = rows // PARTS

    def block(slot, part=0):
        if part == 0:
            return pl.ds(pl.multiple_of(slot * rows, rows), rows)
        return pl.ds(pl.multiple_of(slot * rows + (part - 1) * sub, sub), sub)

    def columns(feature_half):
        return pl.ds(pl.multiple_of(feature_half * half, half), half)

    partner = device(corpus)
    twin = device(1 - 2 * core)
    mine = columns(me_f)
    other = columns(1 - me_f)
    low = here < 2
    high = here >= plane - 2
    back_source = here < 4
    ahead_source = here >= plane - 3
    carries_back = column < 2
    carries = jnp.logical_or(column != 2, core == 1)

    def carrier(p):
        there = p * lanes + 2 * column + core
        return device(there - here + jnp.where(back_source, -plane, plane))

    goal = jnp.where(
        carries_back,
        plane - 2 + core,
        jnp.where(column == 2, 0, core),
    )
    goal_slot = jnp.where(
        carries_back, jnp.where(column == 0, 5, 7), jnp.where(column == 2, 0, 1)
    )
    twice = jnp.logical_or(column == 0, jnp.logical_and(column == 3, core == 1))
    goal_two = jnp.where(column == 0, plane - 4 + core, 2)
    goal_two_slot = jnp.where(column == 0, 7, 0)
    origin = jnp.where(
        carries_back,
        plane + 2 * column + core - here,
        -lanes + 2 * column + core - here,
    )

    def signal(offset):
        pl.semaphore_signal(
            barrier, inc=1, device_id=device(offset), device_id_type=MESH
        )

    barrier = pltpu.get_barrier_semaphore()
    senders = [corpus] + [k + p for p in (corpus, 0) for k in range(-4, 4) if k]
    for offset in senders:
        signal(offset)

    @pl.when(carries)
    def _():
        signal(origin)

    def greet_carriers(place, from_column, from_core):
        def body(p, carry):
            signal(p * lanes + 2 * from_column + from_core - place)
            return carry

        lax.fori_loop(0, PIECES, body, 0)

    @pl.when(high)
    def _():
        greet_carriers(here, 0, core)
        greet_carriers(here, 1, core)

    @pl.when(low)
    def _():
        greet_carriers(here, 3, core)

    @pl.when(here == 0)
    def _():
        greet_carriers(here, 2, 1)

    @pl.when(jnp.logical_and(here >= plane - 4, here < plane - 2))
    def _():
        greet_carriers(here, 0, core)

    @pl.when(here == 2)
    def _():
        greet_carriers(here, 3, 1)

    at_seam = jnp.logical_or(low, high)
    is_source = jnp.logical_or(back_source, ahead_source)
    pl.semaphore_wait(
        barrier,
        len(senders)
        + jnp.where(carries, 1, 0)
        + jnp.where(twice, 1, 0)
        + jnp.where(is_source, PIECES, 0),
    )

    def z_fresh(part):
        return pltpu.make_async_remote_copy(
            src_ref=fresh_ref.at[pl.ds((part - 1) * sub, sub), :],
            dst_ref=blocks.at[block(OWN, part), mine],
            send_sem=zf_send.at[part - 1],
            recv_sem=zf_recv.at[part - 1],
            device_id=partner,
            device_id_type=MESH,
        )


    def z_replay(step):
        at, size = chunks[step]
        return pltpu.make_async_remote_copy(
            src_ref=replay_ref.at[
                pl.ds(pl.multiple_of((1 - me_f) * share + at, size), size), :
            ],
            dst_ref=slab.at[pl.ds(at, size), mine],
            send_sem=zr_send.at[step],
            recv_sem=zr_recv.at[step],
            device_id=partner,
            device_id_type=MESH,
        )

    own_fresh = pltpu.make_async_copy(
        fresh_ref, blocks.at[block(OWN), mine], local_sem.at[0]
    )
    own_replay = pltpu.make_async_copy(
        replay_ref.at[pl.ds(pl.multiple_of(me_f * share, share), share), :],
        slab.at[:, mine],
        local_sem.at[1],
    )

    def spread(part):
        cols = mine if part == 0 else other
        source = fresh_ref if part == 0 else blocks.at[block(OWN, part), cols]

        def to(index, target, slot):
            return pltpu.make_async_remote_copy(
                src_ref=source,
                dst_ref=blocks.at[block(slot, part), cols],
                send_sem=out_send.at[part, index],
                recv_sem=block_recv.at[part, slot],
                device_id=target,
                device_id_type=MESH,
            )

        return [
            (jnp.logical_not(low), to(0, device(-2), 5)),
            (jnp.logical_not(high), to(1, device(2), 1)),
            (None, to(2, twin, 2 + 2 * core)),
        ]

    def edge(p):
        at = pl.ds(pl.multiple_of(p * piece, piece), piece)
        return pltpu.make_async_remote_copy(
            src_ref=fresh_ref.at[at, :],
            dst_ref=carried.at[0],
            send_sem=edge_send.at[p],
            recv_sem=carry_recv.at[0],
            device_id=carrier(p),
            device_id_type=MESH,
        )

    swap = pltpu.make_async_remote_copy(
        src_ref=carried.at[0],
        dst_ref=carried.at[1],
        send_sem=swap_send,
        recv_sem=carry_recv.at[1],
        device_id=partner,
        device_id_type=MESH,
    )

    def feature_half(phase, offset):
        sender = device(offset)[1]
        return columns(sender if phase == 0 else 1 - sender)

    def hand_over(phase):
        def to(index, target, slot):
            at = pl.ds(pl.multiple_of(slot * rows + row * piece, piece), piece)
            return pltpu.make_async_remote_copy(
                src_ref=carried.at[phase],
                dst_ref=blocks.at[at, feature_half(phase, origin)],
                send_sem=carry_send.at[phase, index],
                recv_sem=block_recv.at[
                    0 if phase == 0 else 1 + row * PARTS // PIECES, slot
                ],
                device_id=device(target - here),
                device_id_type=MESH,
            )

        return [
            (carries, to(0, goal, goal_slot)),
            (twice, to(1, goal_two, goal_two_slot)),
        ]

    def passing(part, slot):
        cols = feature_half(min(part, 1), slot - BEHIND)

        def to(index, target, there):
            return pltpu.make_async_remote_copy(
                src_ref=blocks.at[block(slot, part), cols],
                dst_ref=blocks.at[block(there, part), cols],
                send_sem=pass_send.at[part, index],
                recv_sem=block_recv.at[part, there],
                device_id=target,
                device_id_type=MESH,
            )

        if slot == 1:
            onward = jnp.logical_and(core == 1, jnp.logical_not(at_seam))
            return [
                (onward, to(0, device(1), 0)),
                (None, to(1, twin, 2 * core)),
            ]
        if slot == 5:
            return [
                (jnp.logical_not(at_seam), to(2, device(-2), 7)),
                (None, to(3, twin, 4 + 2 * core)),
            ]
        return [(core == 0, to(4, twin, 6))]

    def each(pairs, act):
        for condition, copy in pairs:
            if condition is None:
                act(copy)
            else:
                pl.when(condition)(functools.partial(act, copy))

    def start(copy):
        copy.start()

    def sent(copy):
        copy.wait_send()

    def arrival(part, slot):
        pltpu.make_async_copy(
            blocks.at[block(slot, part), mine],
            blocks.at[block(slot, part), mine],
            block_recv.at[part, slot],
        ).wait()

    def start_edge():
        @pl.when(is_source)
        def _():
            def body(p, carry):
                edge(p).start()
                return carry

            lax.fori_loop(0, PIECES, body, 0)

    def pass_on(part, slot):
        arrival(part, slot)
        each(passing(part, slot), start)

    later = range(1, PARTS + 1)

    def finish_edge():
        @pl.when(is_source)
        def _():
            def body(p, carry):
                edge(p).wait_send()
                return carry

            lax.fori_loop(0, PIECES, body, 0)

        @pl.when(carries)
        def _():
            swap.wait_send()

    z_fresh(1).start()
    start_edge()
    for part in later[1:]:
        z_fresh(part).start()
    each(spread(0), start)
    own_fresh.start()
    own_replay.start()

    fresh_max[...] = jnp.full_like(fresh_max, NEG_FLOOR)
    fresh_sum[...] = jnp.zeros_like(fresh_sum)
    stats[...] = jnp.zeros_like(stats)

    @pl.when(carries)
    def _():
        pltpu.make_async_copy(carried.at[0], carried.at[0], carry_recv.at[0]).wait()
        swap.start()

    each(hand_over(0), start)
    for part in later:
        z_fresh(part).wait_send()
    z_replay(0).start()
    for slot in (1, 5):
        pass_on(0, slot)
    for part in later:
        z_fresh(part).wait_recv()
        each(spread(part), start)
    for step in range(1, len(chunks)):
        z_replay(step).start()

    @pl.when(carries)
    def _():
        swap.wait_recv()

    each(hand_over(1), start)
    pass_on(0, 7)

    for part in later:
        for slot in (1, 5):
            pass_on(part, slot)
    for part in later:
        pass_on(part, 7)

    own_fresh.wait()
    own_replay.wait()

    def score_block(at, size, slot):
        block_rows = block(slot)
        score = (
            lax.dot_general(
                slab[at : at + size, :],
                blocks[block_rows, :],
                (((1,), (1,)), ((), ())),
                preferred_element_type=jnp.float32,
            )
            * scale
        )
        scores[slot, :size, :] = score
        grouped = score.reshape(size // 8, 8, rows)
        old = fresh_max[slot]
        new = jnp.maximum(old, jnp.max(grouped, axis=0))
        fresh_max[slot] = new
        fresh_sum[slot] = fresh_sum[slot] * jnp.exp2(old - new) + jnp.sum(
            jnp.exp2(grouped - new[None]), axis=0
        )

    def finish_rows(at, start_row, size):
        tiles = [
            scores[k, start_row : start_row + size, j : j + 128]
            for k in range(WINDOW)
            for j in range(0, rows, 128)
        ]
        row_max = functools.reduce(jnp.maximum, tiles)
        row_sum = functools.reduce(
            jnp.add, [jnp.exp2(tile - row_max) for tile in tiles]
        )
        row_max = row_max.T
        row_sum = row_sum.T
        top = jnp.max(row_max, axis=0, keepdims=True)
        total = jnp.sum(row_sum * jnp.exp2(row_max - top), axis=0, keepdims=True)
        first = at // 128
        replay_out[first : first + 1, :] = LN2 * (top + jnp.log2(total))

    first_rows = sum(size for _, size in chunks[:first_steps])
    for step in range(first_steps):
        z_replay(step).wait_recv()

    def visit_block(index, carry):
        slot = jnp.where(here < plane // 2, WINDOW - 1 - index, index)

        @pl.when(lax.rem(slot, 2) == 0)
        def _():
            for part in range(PARTS + 1):
                arrival(part, slot)

        score_block(0, first_rows, slot)
        return carry

    lax.fori_loop(0, WINDOW, visit_block, 0)
    for at in range(0, first_rows, 128):
        finish_rows(at, at, 128)

    for step in range(first_steps, len(chunks)):
        at, size = chunks[step]
        z_replay(step).wait_recv()
        for slot in range(WINDOW):
            score_block(at, size, slot)
        if step < len(chunks) - 1:
            for start_row in range(0, size, 128):
                finish_rows(at + start_row, start_row, 128)

    for k in range(WINDOW):
        top = jnp.max(fresh_max[k], axis=0, keepdims=True)
        total = jnp.sum(
            fresh_sum[k] * jnp.exp2(fresh_max[k] - top), axis=0, keepdims=True
        )
        for j in range(rows // 128):
            stats[k, j : j + 1, :] = top[:, j * 128 : (j + 1) * 128]
            stats[k, 2 + j : 3 + j, :] = total[:, j * 128 : (j + 1) * 128]

    def send_stats(k, side):
        return pltpu.make_async_remote_copy(
            src_ref=stats.at[k],
            dst_ref=landed.at[side, k],
            send_sem=stat_send.at[side, k],
            recv_sem=stat_recv.at[side, k],
            device_id=device(k - BEHIND + side * corpus),
            device_id_type=MESH,
        )

    outward = [
        (k, side) for side in (1, 0) for k in range(WINDOW) if side or k != BEHIND
    ]
    for k, side in outward:
        send_stats(k, side).start()
    landed[0, BEHIND] = stats[BEHIND]
    at, size = chunks[-1]
    for start_row in range(0, size, 128):
        finish_rows(at + start_row, start_row, 128)
    finish_edge()
    for phase in (0, 1):
        each(hand_over(phase), sent)
    for part in range(PARTS + 1):
        each(spread(part), sent)
        for slot in (1, 5, 7):
            each(passing(part, slot), sent)
    for step in range(len(chunks)):
        z_replay(step).wait_send()
    for k, side in outward:
        send_stats(k, side).wait()
    got = landed[...].reshape(2 * WINDOW, 8, 128)
    top = jnp.max(got[:, 0:2, :], axis=0)
    total = jnp.sum(got[:, 2:4, :] * jnp.exp2(got[:, 0:2, :] - top[None]), axis=0)
    fresh_out[...] = LN2 * (top + jnp.log2(total))


def per_device(corpus, plane, fresh_embed, replay_embed):
    rows, half = fresh_embed.shape
    share = replay_embed.shape[0] // 2
    sizes = (256, 256, 256, 128, 128)
    chunks = [(sum(sizes[:i]), size) for i, size in enumerate(sizes)]
    first_steps = 2
    most = max(sum(sizes[:first_steps]), max(sizes))
    full = 2 * half
    scale = 0.25 / math.sqrt(full) * math.log2(math.e)
    dma = pltpu.SemaphoreType.DMA
    fresh_lse, replay_lse = pl.pallas_call(
        functools.partial(kernel, corpus, plane, chunks, first_steps, scale),
        out_shape=(
            jax.ShapeDtypeStruct((rows // 128, 128), jnp.float32),
            jax.ShapeDtypeStruct((share // 128, 128), jnp.float32),
        ),
        in_specs=[pl.BlockSpec(memory_space=pltpu.HBM)] * 2,
        out_specs=[pl.BlockSpec(memory_space=pltpu.VMEM)] * 2,
        scratch_shapes=[
            pltpu.VMEM((WINDOW * rows, full), jnp.bfloat16),
            pltpu.VMEM((share, full), jnp.bfloat16),
            pltpu.VMEM((WINDOW, most, rows), jnp.float32),
            pltpu.VMEM((WINDOW, 8, rows), jnp.float32),
            pltpu.VMEM((WINDOW, 8, rows), jnp.float32),
            pltpu.VMEM((WINDOW, 8, 128), jnp.float32),
            pltpu.VMEM((2, WINDOW, 8, 128), jnp.float32),
            pltpu.VMEM((2, rows // PIECES, half), jnp.bfloat16),
            dma((2,)),
            dma((PARTS,)),
            dma((PARTS,)),
            dma((len(chunks),)),
            dma((len(chunks),)),
            dma((PARTS + 1, 3)),
            dma((PARTS + 1, 5)),
            dma((PIECES,)),
            dma((PARTS + 1, WINDOW)),
            dma,
            dma((2, 2)),
            dma((2,)),
            dma((2, WINDOW)),
            dma((2, WINDOW)),
        ],
        compiler_params=pltpu.CompilerParams(
            collective_id=0, has_side_effects=True, vmem_limit_bytes=VMEM_BYTES
        ),
    )(fresh_embed, replay_embed)
    return fresh_lse.reshape(rows), replay_lse.reshape(share)


def solution(mesh):
    placed = (P("corpus", "feat"), P("corpus", "feat"))
    return jax.shard_map(
        functools.partial(per_device, mesh.shape["corpus"], PLANE),
        mesh=mesh,
        in_specs=placed,
        out_specs=(P("corpus"), P(("corpus", "feat"))),
        check_vma=False,
    )
```

```python
import functools
import math

import jax
import jax.numpy as jnp
from jax import lax
from jax.experimental import pallas as pl
from jax.experimental.pallas import tpu as pltpu
from jax.sharding import PartitionSpec as P

MESH = pl.DeviceIdType.MESH
WINDOW = 8
BEHIND = 3
OWN = 3
PLANE = 64
PIECES = 8
NEG_FLOOR = -1e30
LN2 = math.log(2.0)
VMEM_BYTES = 55104 * 1024
PARTS = 2


def kernel(
    corpus,
    plane,
    chunks,
    first_steps,
    scale,
    fresh_ref,
    replay_ref,
    fresh_out,
    replay_out,
    blocks,
    slab,
    scores,
    fresh_max,
    fresh_sum,
    stats,
    landed,
    carried,
    local_sem,
    zf_send,
    zf_recv,
    zr_send,
    zr_recv,
    out_send,
    pass_send,
    edge_send,
    block_recv,
    swap_send,
    carry_send,
    carry_recv,
    stat_send,
    stat_recv,
):
    rows, half = fresh_ref.shape
    share = replay_ref.shape[0] // 2
    lanes = plane // PIECES
    piece = rows // PIECES
    me_c = lax.axis_index("corpus")
    me_f = lax.axis_index("feat")
    ring = 2 * corpus
    me = me_f * corpus + me_c
    here = lax.rem(me_c, plane)
    core = lax.rem(here, 2)
    column = lax.rem(here, lanes) // 2
    row = here // lanes

    def device(offset):
        there = lax.rem(me + offset + ring, ring)
        return (lax.rem(there, corpus), there // corpus)

    sub = rows // PARTS

    def block(slot, part=0):
        if part == 0:
            return pl.ds(pl.multiple_of(slot * rows, rows), rows)
        return pl.ds(pl.multiple_of(slot * rows + (part - 1) * sub, sub), sub)

    def columns(feature_half):
        return pl.ds(pl.multiple_of(feature_half * half, half), half)

    partner = device(corpus)
    twin = device(1 - 2 * core)
    mine = columns(me_f)
    other = columns(1 - me_f)
    low = here < 2
    high = here >= plane - 2
    back_source = here < 4
    ahead_source = here >= plane - 3
    carries_back = column < 2
    carries = jnp.logical_or(column != 2, core == 1)

    def carrier(p):
        there = p * lanes + 2 * column + core
        return device(there - here + jnp.where(back_source, -plane, plane))

    goal = jnp.where(
        carries_back,
        plane - 2 + core,
        jnp.where(column == 2, 0, core),
    )
    goal_slot = jnp.where(
        carries_back, jnp.where(column == 0, 5, 7), jnp.where(column == 2, 0, 1)
    )
    twice = jnp.logical_or(column == 0, jnp.logical_and(column == 3, core == 1))
    goal_two = jnp.where(column == 0, plane - 4 + core, 2)
    goal_two_slot = jnp.where(column == 0, 7, 0)
    origin = jnp.where(
        carries_back,
        plane + 2 * column + core - here,
        -lanes + 2 * column + core - here,
    )

    def signal(offset):
        pl.semaphore_signal(
            barrier, inc=1, device_id=device(offset), device_id_type=MESH
        )

    barrier = pltpu.get_barrier_semaphore()
    senders = [corpus] + [k + p for p in (corpus, 0) for k in range(-4, 4) if k]
    for offset in senders:
        signal(offset)

    @pl.when(carries)
    def _():
        signal(origin)

    def greet_carriers(place, from_column, from_core):
        def body(p, carry):
            signal(p * lanes + 2 * from_column + from_core - place)
            return carry

        lax.fori_loop(0, PIECES, body, 0)

    @pl.when(high)
    def _():
        greet_carriers(here, 0, core)
        greet_carriers(here, 1, core)

    @pl.when(low)
    def _():
        greet_carriers(here, 3, core)

    @pl.when(here == 0)
    def _():
        greet_carriers(here, 2, 1)

    @pl.when(jnp.logical_and(here >= plane - 4, here < plane - 2))
    def _():
        greet_carriers(here, 0, core)

    @pl.when(here == 2)
    def _():
        greet_carriers(here, 3, 1)

    at_seam = jnp.logical_or(low, high)
    is_source = jnp.logical_or(back_source, ahead_source)
    pl.semaphore_wait(
        barrier,
        len(senders)
        + jnp.where(carries, 1, 0)
        + jnp.where(twice, 1, 0)
        + jnp.where(is_source, PIECES, 0),
    )

    def z_fresh(part):
        return pltpu.make_async_remote_copy(
            src_ref=fresh_ref.at[pl.ds((part - 1) * sub, sub), :],
            dst_ref=blocks.at[block(OWN, part), mine],
            send_sem=zf_send.at[part - 1],
            recv_sem=zf_recv.at[part - 1],
            device_id=partner,
            device_id_type=MESH,
        )


    def z_replay(step):
        at, size = chunks[step]
        return pltpu.make_async_remote_copy(
            src_ref=replay_ref.at[
                pl.ds(pl.multiple_of((1 - me_f) * share + at, size), size), :
            ],
            dst_ref=slab.at[pl.ds(at, size), mine],
            send_sem=zr_send.at[step],
            recv_sem=zr_recv.at[step],
            device_id=partner,
            device_id_type=MESH,
        )

    own_fresh = pltpu.make_async_copy(
        fresh_ref, blocks.at[block(OWN), mine], local_sem.at[0]
    )
    own_replay = pltpu.make_async_copy(
        replay_ref.at[pl.ds(pl.multiple_of(me_f * share, share), share), :],
        slab.at[:, mine],
        local_sem.at[1],
    )

    def spread(part):
        cols = mine if part == 0 else other
        source = fresh_ref if part == 0 else blocks.at[block(OWN, part), cols]

        def to(index, target, slot):
            return pltpu.make_async_remote_copy(
                src_ref=source,
                dst_ref=blocks.at[block(slot, part), cols],
                send_sem=out_send.at[part, index],
                recv_sem=block_recv.at[part, slot],
                device_id=target,
                device_id_type=MESH,
            )

        return [
            (jnp.logical_not(low), to(0, device(-2), 5)),
            (jnp.logical_not(high), to(1, device(2), 1)),
            (None, to(2, twin, 2 + 2 * core)),
        ]

    def edge(p):
        at = pl.ds(pl.multiple_of(p * piece, piece), piece)
        return pltpu.make_async_remote_copy(
            src_ref=fresh_ref.at[at, :],
            dst_ref=carried.at[0],
            send_sem=edge_send.at[p],
            recv_sem=carry_recv.at[0],
            device_id=carrier(p),
            device_id_type=MESH,
        )

    swap = pltpu.make_async_remote_copy(
        src_ref=carried.at[0],
        dst_ref=carried.at[1],
        send_sem=swap_send,
        recv_sem=carry_recv.at[1],
        device_id=partner,
        device_id_type=MESH,
    )

    def feature_half(phase, offset):
        sender = device(offset)[1]
        return columns(sender if phase == 0 else 1 - sender)

    def hand_over(phase):
        def to(index, target, slot):
            at = pl.ds(pl.multiple_of(slot * rows + row * piece, piece), piece)
            return pltpu.make_async_remote_copy(
                src_ref=carried.at[phase],
                dst_ref=blocks.at[at, feature_half(phase, origin)],
                send_sem=carry_send.at[phase, index],
                recv_sem=block_recv.at[
                    0 if phase == 0 else 1 + row * PARTS // PIECES, slot
                ],
                device_id=device(target - here),
                device_id_type=MESH,
            )

        return [
            (carries, to(0, goal, goal_slot)),
            (twice, to(1, goal_two, goal_two_slot)),
        ]

    def passing(part, slot):
        cols = feature_half(min(part, 1), slot - BEHIND)

        def to(index, target, there):
            return pltpu.make_async_remote_copy(
                src_ref=blocks.at[block(slot, part), cols],
                dst_ref=blocks.at[block(there, part), cols],
                send_sem=pass_send.at[part, index],
                recv_sem=block_recv.at[part, there],
                device_id=target,
                device_id_type=MESH,
            )

        if slot == 1:
            onward = jnp.logical_and(core == 1, jnp.logical_not(at_seam))
            return [
                (onward, to(0, device(1), 0)),
                (None, to(1, twin, 2 * core)),
            ]
        if slot == 5:
            return [
                (jnp.logical_not(at_seam), to(2, device(-2), 7)),
                (None, to(3, twin, 4 + 2 * core)),
            ]
        return [(core == 0, to(4, twin, 6))]

    def each(pairs, act):
        for condition, copy in pairs:
            if condition is None:
                act(copy)
            else:
                pl.when(condition)(functools.partial(act, copy))

    def start(copy):
        copy.start()

    def sent(copy):
        copy.wait_send()

    def arrival(part, slot):
        pltpu.make_async_copy(
            blocks.at[block(slot, part), mine],
            blocks.at[block(slot, part), mine],
            block_recv.at[part, slot],
        ).wait()

    def start_edge():
        @pl.when(is_source)
        def _():
            def body(p, carry):
                edge(p).start()
                return carry

            lax.fori_loop(0, PIECES, body, 0)

    def pass_on(part, slot):
        arrival(part, slot)
        each(passing(part, slot), start)

    later = range(1, PARTS + 1)

    def finish_edge():
        @pl.when(is_source)
        def _():
            def body(p, carry):
                edge(p).wait_send()
                return carry

            lax.fori_loop(0, PIECES, body, 0)

        @pl.when(carries)
        def _():
            swap.wait_send()

    z_fresh(1).start()
    start_edge()
    for part in later[1:]:
        z_fresh(part).start()
    each(spread(0), start)
    own_fresh.start()
    own_replay.start()

    fresh_max[...] = jnp.full_like(fresh_max, NEG_FLOOR)
    fresh_sum[...] = jnp.zeros_like(fresh_sum)
    stats[...] = jnp.zeros_like(stats)

    @pl.when(carries)
    def _():
        pltpu.make_async_copy(carried.at[0], carried.at[0], carry_recv.at[0]).wait()
        swap.start()

    each(hand_over(0), start)
    for part in later:
        z_fresh(part).wait_send()
    for step in range(2):
        z_replay(step).start()
    for slot in (1, 5):
        pass_on(0, slot)
    for part in later:
        z_fresh(part).wait_recv()
        each(spread(part), start)
    for step in range(2, len(chunks)):
        z_replay(step).start()

    @pl.when(carries)
    def _():
        swap.wait_recv()

    each(hand_over(1), start)
    pass_on(0, 7)

    for part in later:
        for slot in (1, 5):
            pass_on(part, slot)
    for part in later:
        pass_on(part, 7)

    own_fresh.wait()
    own_replay.wait()

    def score_block(at, size, slot):
        block_rows = block(slot)
        score = (
            lax.dot_general(
                slab[at : at + size, :],
                blocks[block_rows, :],
                (((1,), (1,)), ((), ())),
                preferred_element_type=jnp.float32,
            )
            * scale
        )
        scores[slot, :size, :] = score
        grouped = score.reshape(size // 8, 8, rows)
        old = fresh_max[slot]
        new = jnp.maximum(old, jnp.max(grouped, axis=0))
        fresh_max[slot] = new
        fresh_sum[slot] = fresh_sum[slot] * jnp.exp2(old - new) + jnp.sum(
            jnp.exp2(grouped - new[None]), axis=0
        )

    def finish_rows(at, start_row, size):
        tiles = [
            scores[k, start_row : start_row + size, j : j + 128]
            for k in range(WINDOW)
            for j in range(0, rows, 128)
        ]
        row_max = functools.reduce(jnp.maximum, tiles)
        row_sum = functools.reduce(
            jnp.add, [jnp.exp2(tile - row_max) for tile in tiles]
        )
        row_max = row_max.T
        row_sum = row_sum.T
        top = jnp.max(row_max, axis=0, keepdims=True)
        total = jnp.sum(row_sum * jnp.exp2(row_max - top), axis=0, keepdims=True)
        first = at // 128
        replay_out[first : first + 1, :] = LN2 * (top + jnp.log2(total))

    first_rows = sum(size for _, size in chunks[:first_steps])
    for step in range(first_steps):
        z_replay(step).wait_recv()

    def visit_block(index, carry):
        slot = jnp.where(here < plane // 2, WINDOW - 1 - index, index)

        @pl.when(lax.rem(slot, 2) == 0)
        def _():
            for part in range(PARTS + 1):
                arrival(part, slot)

        score_block(0, first_rows, slot)
        return carry

    lax.fori_loop(0, WINDOW, visit_block, 0)
    for at in range(0, first_rows, 128):
        finish_rows(at, at, 128)

    for step in range(first_steps, len(chunks)):
        at, size = chunks[step]
        z_replay(step).wait_recv()
        for slot in range(WINDOW):
            score_block(at, size, slot)
        if step < len(chunks) - 1:
            for start_row in range(0, size, 128):
                finish_rows(at + start_row, start_row, 128)

    for k in range(WINDOW):
        top = jnp.max(fresh_max[k], axis=0, keepdims=True)
        total = jnp.sum(
            fresh_sum[k] * jnp.exp2(fresh_max[k] - top), axis=0, keepdims=True
        )
        for j in range(rows // 128):
            stats[k, j : j + 1, :] = top[:, j * 128 : (j + 1) * 128]
            stats[k, 2 + j : 3 + j, :] = total[:, j * 128 : (j + 1) * 128]

    def send_stats(k, side):
        return pltpu.make_async_remote_copy(
            src_ref=stats.at[k],
            dst_ref=landed.at[side, k],
            send_sem=stat_send.at[side, k],
            recv_sem=stat_recv.at[side, k],
            device_id=device(k - BEHIND + side * corpus),
            device_id_type=MESH,
        )

    outward = [
        (k, side) for side in (1, 0) for k in range(WINDOW) if side or k != BEHIND
    ]
    for k, side in outward:
        send_stats(k, side).start()
    landed[0, BEHIND] = stats[BEHIND]
    at, size = chunks[-1]
    for start_row in range(0, size, 128):
        finish_rows(at + start_row, start_row, 128)
    finish_edge()
    for phase in (0, 1):
        each(hand_over(phase), sent)
    for part in range(PARTS + 1):
        each(spread(part), sent)
        for slot in (1, 5, 7):
            each(passing(part, slot), sent)
    for step in range(len(chunks)):
        z_replay(step).wait_send()
    for k, side in outward:
        send_stats(k, side).wait()
    got = landed[...].reshape(2 * WINDOW, 8, 128)
    top = jnp.max(got[:, 0:2, :], axis=0)
    total = jnp.sum(got[:, 2:4, :] * jnp.exp2(got[:, 0:2, :] - top[None]), axis=0)
    fresh_out[...] = LN2 * (top + jnp.log2(total))


def per_device(corpus, plane, fresh_embed, replay_embed):
    rows, half = fresh_embed.shape
    share = replay_embed.shape[0] // 2
    sizes = (256, 256, 256, 128, 128)
    chunks = [(sum(sizes[:i]), size) for i, size in enumerate(sizes)]
    first_steps = 2
    most = max(sum(sizes[:first_steps]), max(sizes))
    full = 2 * half
    scale = 0.25 / math.sqrt(full) * math.log2(math.e)
    dma = pltpu.SemaphoreType.DMA
    fresh_lse, replay_lse = pl.pallas_call(
        functools.partial(kernel, corpus, plane, chunks, first_steps, scale),
        out_shape=(
            jax.ShapeDtypeStruct((rows // 128, 128), jnp.float32),
            jax.ShapeDtypeStruct((share // 128, 128), jnp.float32),
        ),
        in_specs=[pl.BlockSpec(memory_space=pltpu.HBM)] * 2,
        out_specs=[pl.BlockSpec(memory_space=pltpu.VMEM)] * 2,
        scratch_shapes=[
            pltpu.VMEM((WINDOW * rows, full), jnp.bfloat16),
            pltpu.VMEM((share, full), jnp.bfloat16),
            pltpu.VMEM((WINDOW, most, rows), jnp.float32),
            pltpu.VMEM((WINDOW, 8, rows), jnp.float32),
            pltpu.VMEM((WINDOW, 8, rows), jnp.float32),
            pltpu.VMEM((WINDOW, 8, 128), jnp.float32),
            pltpu.VMEM((2, WINDOW, 8, 128), jnp.float32),
            pltpu.VMEM((2, rows // PIECES, half), jnp.bfloat16),
            dma((2,)),
            dma((PARTS,)),
            dma((PARTS,)),
            dma((len(chunks),)),
            dma((len(chunks),)),
            dma((PARTS + 1, 3)),
            dma((PARTS + 1, 5)),
            dma((PIECES,)),
            dma((PARTS + 1, WINDOW)),
            dma,
            dma((2, 2)),
            dma((2,)),
            dma((2, WINDOW)),
            dma((2, WINDOW)),
        ],
        compiler_params=pltpu.CompilerParams(
            collective_id=0, has_side_effects=True, vmem_limit_bytes=VMEM_BYTES
        ),
    )(fresh_embed, replay_embed)
    return fresh_lse.reshape(rows), replay_lse.reshape(share)


def solution(mesh):
    placed = (P("corpus", "feat"), P("corpus", "feat"))
    return jax.shard_map(
        functools.partial(per_device, mesh.shape["corpus"], PLANE),
        mesh=mesh,
        in_specs=placed,
        out_specs=(P("corpus"), P(("corpus", "feat"))),
        check_vma=False,
    )
```
